32 devices in a mesh: dp: 4 (over z), section: 2 (over x), expert: 4 (over y, core).
Axes of the slice: x: 2, y: 2, z: 4, core: 2. Of those that a mesh axis runs over, the one named last changes fastest.
Arguments:
- act_in: bfloat16 [2, 1024, 2048], P('section', ('dp', 'expert')), may hold values from -6 to 6
- saved_in: bfloat16 [2, 1024, 2048], P('section', ('dp', 'expert')), may hold values from -6 to 6
- grad_in: bfloat16 [2, 1024, 2048], P('section', ('dp', 'expert')), may hold values from -6 to 6
- fwd_ids: int32 [2, 1024, 2], P('section', ('dp', 'expert')), may hold values from 0 to 3, all different within a row; in each aligned block of 64 rows (0 to 63, 64 to 127, ..., all dimensions but the last counted through in order) at most 40 rows name the same one
- bwd_ids: int32 [2, 1024, 2], P('section', ('dp', 'expert')), may hold values from 0 to 3, all different within a row; in each aligned block of 64 rows (0 to 63, 64 to 127, ..., all dimensions but the last counted through in order) at most 40 rows name the same one
- fwd_gates: float32 [2, 1024, 2], P('section', ('dp', 'expert')), may hold values from 0.2 to 1
- bwd_gates: float32 [2, 1024, 2], P('section', ('dp', 'expert')), may hold values from 0.2 to 1
- norm_gain: float32 [2, 2048], P('section'), may hold values from 0.5 to 1.5
- w_gate: bfloat16 [2, 4, 2048, 384], P('section', 'expert'), may hold values from -0.125 to 0.125
- w_up: bfloat16 [2, 4, 2048, 384], P('section', 'expert'), may hold values from -0.125 to 0.125
- w_down: bfloat16 [2, 4, 384, 2048], P('section', 'expert'), may hold values from -0.3125 to 0.3125
Outputs:
- act_out: bfloat16 [2, 1024, 2048], P('section', ('dp', 'expert'))
- grad_out: bfloat16 [2, 1024, 2048], P('section', ('dp', 'expert'))
- weight_grads: float32 [2, 4, 2048, 1152], P('section', 'expert', 'dp')
The draws below stay inside these ranges and needn't reach their ends.
Inputs may be any that keep to these rules, and one draw needn't show every extreme that they name: `fwd_ids`: the 2 entries of a token name different experts. In each aligned block of 64 tokens of a section (the tokens of one device), no expert is named by more than 40 entries, and in every draw some block has an expert named exactly 40 times. `bwd_ids`: the 2 entries of a token name different experts. In each aligned block of 64 tokens of a section (the tokens of one device), no expert is named by more than 40 entries, and in every draw some block has an expert named exactly 40 times.
All inputs are finite; a program needn't handle non-finite values.
Results may differ from the reference program's by a relative error of at most 0.017.
Values may be sent and summed in bfloat16 or wider, within the bound.
A program may use at most 64 MiB of HBM per device.

```python
import math
import jax
import jax.numpy as jnp
import numpy as np
from jax import lax

D = 2048
HID = 384
TOPK = 2
TOK_DEV = 64
EXPERTS = 4
CAP = 40
TOKENS = 1024
N_DP = 4
N_SECTION = 2
N_EXPERT = 4


def block_scale(stream_key, dims, pieces, least, high):
    factor_of, own = 1.0, jax.random.fold_in(stream_key, 6)
    for axis_at, parts in pieces:
        draws = jnp.exp(jax.random.uniform(jax.random.fold_in(own, axis_at), (parts,), jnp.float32, least / len(pieces), high / len(pieces)))
        factor_of = factor_of * jnp.repeat(draws, dims[axis_at] // parts).reshape([-1 if axis == axis_at else 1 for axis in range(len(dims))])
    return factor_of


def routed_block(own_key, own, number, rows, number_of, top, most, slope):
    sequence = jax.random.permutation(own_key, number_of)
    crowded, ordinary = load_shares(number_of, rows * top, most, slope, True), load_shares(number_of, rows * top, most, slope, False)
    places = jnp.arange(number_of)

    def named(tallies, rotation):
        used = int((tallies > 0).sum())
        fixed = max(1, used // 4)
        passed = fixed + (places - fixed + rotation * (used - fixed)) % max(1, number_of - fixed)
        return jnp.zeros((number_of,), jnp.int32).at[sequence[jnp.where(places < fixed, places, passed)]].set(jnp.asarray(tallies, jnp.int32))

    tallies = jnp.where(number % 4 == 0, named(crowded, number // 4), named(ordinary, number - number // 4 - 1))
    mixed = jax.random.permutation(jax.random.fold_in(own, 3), number_of)
    source_of, sink = mixed[0:number_of // 2 * 2:2], mixed[1:number_of // 2 * 2:2]
    slack = jnp.minimum(tallies[source_of] - 1, most - tallies[sink]) // 2
    slack = jnp.where((source_of == sequence[0]) | (sink == sequence[0]) | (tallies[sink] == 0), 0, jnp.maximum(slack, 0))
    passed = jax.random.randint(jax.random.fold_in(own, 4), (number_of // 2,), 0, 1 << 20) % (slack + 1)
    tallies = tallies.at[source_of].add(-passed).at[sink].add(passed)
    members = jnp.searchsorted(jnp.cumsum(tallies), jnp.arange(rows * top), side="right").astype(jnp.int32)
    table = members.reshape(top, rows).T
    table = table[jax.random.permutation(jax.random.fold_in(own, 1), rows)]
    rotation = jax.random.randint(jax.random.fold_in(own, 2), (rows, 1), 0, top)
    return jnp.take_along_axis(table, (jnp.arange(top)[None, :] + rotation) % top, axis=1)


def load_shares(amount, total, reach, lean, full):
    portions = [(1 << 20) // math.isqrt(rank ** lean) + 1 for rank in range(1, amount + 1)]
    largest = reach if full else min(reach, max(-(-total // amount), total * portions[0] // sum(portions)))
    least = 1 if total - largest >= amount - 1 else 0
    counts, surplus = [largest] + [least] * (amount - 1), total - largest - least * (amount - 1)
    while surplus > 0:
        free = [i for i in range(1, amount) if counts[i] < largest] or [i for i in range(1, amount) if counts[i] < reach]
        pool, remaining = sum([portions[i] for i in free]), surplus
        for i in free:
            more = min(reach - counts[i], max(1, remaining * portions[i] // pool), surplus)
            counts[i] = counts[i] + more
            surplus = surplus - more
    return np.array(counts)


def bell_draw(rng, extent, spread, most, pieces=(), kind=jnp.bfloat16):
    entries = spread * jax.random.normal(rng, extent, jnp.float32)
    if pieces:
        entries = entries * block_scale(rng, extent, pieces, -0.22, 0.18)
    return jnp.clip(entries, -most, most).astype(kind)


def setup_inputs(seed: int = 0) -> dict:
    streams_of = jax.random.split(jax.random.key(seed), 12)
    act_in = bell_draw(streams_of[0], (N_SECTION, TOKENS, D), 1.0, 6.0, ((0, 2), (1, 16)))
    saved_in = bell_draw(streams_of[1], (N_SECTION, TOKENS, D), 1.0, 6.0, ((0, 2), (1, 16)))
    grad_in = bell_draw(streams_of[2], (N_SECTION, TOKENS, D), 1.0, 6.0, ((0, 2), (1, 16)))
    fwd_ids_keys = jax.random.split(jax.random.fold_in(streams_of[3], 1), N_SECTION * TOKENS // TOK_DEV)
    fwd_ids_turns = jax.random.permutation(jax.random.fold_in(streams_of[3], 3), N_SECTION * TOKENS // TOK_DEV)
    fwd_ids = jax.vmap(lambda own, number: routed_block(jax.random.fold_in(streams_of[3], 2), own, number, TOK_DEV, EXPERTS, TOPK, CAP, 1))(fwd_ids_keys, fwd_ids_turns).reshape((N_SECTION, TOKENS, TOPK))
    bwd_ids_keys = jax.random.split(jax.random.fold_in(streams_of[4], 1), N_SECTION * TOKENS // TOK_DEV)
    bwd_ids_turns = jax.random.permutation(jax.random.fold_in(streams_of[4], 3), N_SECTION * TOKENS // TOK_DEV)
    bwd_ids = jax.vmap(lambda own, number: routed_block(jax.random.fold_in(streams_of[4], 2), own, number, TOK_DEV, EXPERTS, TOPK, CAP, 1))(bwd_ids_keys, bwd_ids_turns).reshape((N_SECTION, TOKENS, TOPK))
    fwd_gates = jnp.clip(jnp.exp(math.log(1.0) - 1.609438 * jax.random.uniform(streams_of[5], (N_SECTION, TOKENS, TOPK), jnp.float32) ** block_scale(streams_of[5], (N_SECTION, TOKENS, TOPK), ((0, 2), (1, 16)), -0.2, 0.2)), 0.2, 1.0)
    bwd_gates = jnp.clip(jnp.exp(math.log(1.0) - 1.609438 * jax.random.uniform(streams_of[6], (N_SECTION, TOKENS, TOPK), jnp.float32) ** block_scale(streams_of[6], (N_SECTION, TOKENS, TOPK), ((0, 2), (1, 16)), -0.2, 0.2)), 0.2, 1.0)
    norm_gain = jnp.clip(1.0 + 0.1 * jax.random.normal(streams_of[7], (N_SECTION, D), jnp.float32), 0.5, 1.5)
    w_gate = bell_draw(streams_of[8], (N_SECTION, EXPERTS, D, HID), D ** -0.5, 0.125, ((0, 2), (1, 4)))
    w_up = bell_draw(streams_of[9], (N_SECTION, EXPERTS, D, HID), D ** -0.5, 0.125, ((0, 2), (1, 4)))
    w_down = bell_draw(streams_of[10], (N_SECTION, EXPERTS, HID, D), HID ** -0.5, 0.3125, ((0, 2), (1, 4)))
    return {"act_in": act_in, "saved_in": saved_in, "grad_in": grad_in, "fwd_ids": fwd_ids, "bwd_ids": bwd_ids, "fwd_gates": fwd_gates, "bwd_gates": bwd_gates, "norm_gain": norm_gain, "w_gate": w_gate, "w_up": w_up, "w_down": w_down}


EPS = 1e-06

def rms_norm(rows, gain):
    wide = rows.astype(jnp.float32)
    factor = lax.rsqrt(lax.optimization_barrier(jnp.mean(wide * wide, axis=-1, keepdims=True)) + EPS)
    return wide * factor * gain

def slot_numbers(ids):
    blocks = ids.reshape(-1, TOK_DEV * TOPK)
    onehot = (blocks[:, :, None] == jnp.arange(EXPERTS, dtype=jnp.int32)[None, None, :]).astype(jnp.int32)
    before = jnp.cumsum(onehot, axis=1) - onehot
    return lax.optimization_barrier(jnp.sum(before * onehot, axis=2)).reshape(ids.shape).astype(jnp.int32)

def owners():
    return (jnp.arange(TOKENS, dtype=jnp.int32) // TOK_DEV)[:, None] + jnp.zeros((1, TOPK), jnp.int32)

def pack(values, ids, slots):
    empty = jnp.zeros((EXPERTS, N_DP * N_EXPERT, CAP, values.shape[-1]), values.dtype)
    return empty.at[ids, owners(), slots].set(values)

def unpack(packed, ids, slots):
    return packed[ids, owners(), slots]

def expert_forward(args):
    rows, w_g, w_u, w_d = args
    flat = rows.reshape(-1, rows.shape[-1])
    pre_gate = jnp.dot(flat, w_g, preferred_element_type=jnp.float32)
    pre_up = jnp.dot(flat, w_u, preferred_element_type=jnp.float32)
    hidden = (jax.nn.silu(pre_gate) * pre_up).astype(jnp.bfloat16)
    produced = jnp.dot(hidden, w_d, preferred_element_type=jnp.float32).astype(jnp.bfloat16)
    return produced.reshape(rows.shape)

def expert_backward(args):
    rows, grads, w_g, w_u, w_d = args
    flat = rows.reshape(-1, rows.shape[-1])
    flat_grad = grads.reshape(-1, grads.shape[-1])
    pre_gate = jnp.dot(flat, w_g, preferred_element_type=jnp.float32)
    pre_up = jnp.dot(flat, w_u, preferred_element_type=jnp.float32)
    sig = jax.nn.sigmoid(pre_gate)
    silu_gate = jax.nn.silu(pre_gate)
    hidden = (silu_gate * pre_up).astype(jnp.bfloat16)
    hidden_grad = jnp.dot(flat_grad, w_d.T, preferred_element_type=jnp.float32)
    gate_grad = (hidden_grad * pre_up * sig * (1.0 + pre_gate * (1.0 - sig))).astype(jnp.bfloat16)
    up_grad = (hidden_grad * silu_gate).astype(jnp.bfloat16)
    slot_grad = (jnp.dot(gate_grad, w_g.T, preferred_element_type=jnp.float32) + jnp.dot(up_grad, w_u.T, preferred_element_type=jnp.float32)).astype(jnp.bfloat16)

    def per_replica(matrix):
        return matrix.reshape(N_DP, -1, matrix.shape[-1]).astype(jnp.float32)
    inputs_r = per_replica(flat)
    part_gate = jnp.einsum('rnk,rnh->rkh', inputs_r, per_replica(gate_grad))
    part_up = jnp.einsum('rnk,rnh->rkh', inputs_r, per_replica(up_grad))
    part_down = jnp.einsum('rnk,rnh->rkh', per_replica(flat_grad), per_replica(hidden))
    partial_value = (jnp.concatenate([part_gate, part_up, part_down], axis=2) / N_DP).astype(jnp.bfloat16)
    total = lax.optimization_barrier(jnp.sum(partial_value.astype(jnp.float32), axis=0))
    return (slot_grad.reshape(rows.shape), total)

def reference(act_in, saved_in, grad_in, fwd_ids, bwd_ids, fwd_gates, bwd_gates, norm_gain, w_gate, w_up, w_down):
    layer_outs = []
    input_grads = []
    weight_list = []
    for section in range(N_SECTION):
        gain = norm_gain[section]
        here = act_in[section]
        normed = rms_norm(here, gain).astype(jnp.bfloat16)
        slots = slot_numbers(fwd_ids[section])
        packed = pack(jnp.broadcast_to(normed[:, None, :], (TOKENS, TOPK, D)), fwd_ids[section], slots)
        produced = lax.map(expert_forward, (packed, w_gate[section], w_up[section], w_down[section]))
        gathered = unpack(produced, fwd_ids[section], slots).astype(jnp.float32)
        layer_out = (here.astype(jnp.float32) + lax.optimization_barrier(jnp.sum(fwd_gates[section][:, :, None] * gathered, axis=1))).astype(jnp.bfloat16)
        layer_outs.append(layer_out)
        saved_wide = saved_in[section].astype(jnp.float32)
        normed_wide, pull_back = jax.vjp(lambda v: rms_norm(v, gain), saved_wide)
        normed_bwd = normed_wide.astype(jnp.bfloat16)
        upstream = grad_in[section].astype(jnp.float32)
        out_grad = (bwd_gates[section][:, :, None] * upstream[:, None, :]).astype(jnp.bfloat16)
        back_slots = slot_numbers(bwd_ids[section])
        packed_in = pack(jnp.broadcast_to(normed_bwd[:, None, :], (TOKENS, TOPK, D)), bwd_ids[section], back_slots)
        packed_grad = pack(out_grad, bwd_ids[section], back_slots)
        slot_grad, totals = lax.map(expert_backward, (packed_in, packed_grad, w_gate[section], w_up[section], w_down[section]))
        normed_grad = lax.optimization_barrier(jnp.sum(unpack(slot_grad, bwd_ids[section], back_slots).astype(jnp.float32), axis=1))
        input_grad = (upstream + pull_back(normed_grad)[0]).astype(jnp.bfloat16)
        input_grads.append(input_grad)
        weight_list.append(totals)
    act_out = jnp.roll(jnp.stack(layer_outs), 1, axis=0)
    grad_out = jnp.roll(jnp.stack(input_grads), -1, axis=0)
    return (act_out, grad_out, jnp.stack(weight_list))
```

```python
import functools

import jax
import jax.numpy as jnp
from jax import lax
from jax.experimental import pallas as pl
from jax.experimental.pallas import tpu as pltpu
from jax.sharding import PartitionSpec as P

EPS = 1e-06
MESH = pl.DeviceIdType.MESH
F32 = jnp.float32
BF16 = jnp.bfloat16
LAST = (((1,), (1,)), ((), ()))
FIRST = (((0,), (0,)), ((), ()))


def bits_of(n):
    return [1 << b for b in reversed(range(n.bit_length() - 1))]


def lowest(m):
    return m & -m


def arrival_order(n):
    return sorted(range(1, n), key=lambda m: (-lowest(m), m))


class Copies:
    def __init__(self, send, recv):
        self.send, self.recv, self.names = send, recv, {}

    def make(self, name, src, dst, peer):
        i = self.names.setdefault(name, len(self.names))
        return pltpu.make_async_remote_copy(
            src_ref=src,
            dst_ref=dst,
            send_sem=self.send.at[i],
            recv_sem=self.recv.at[i],
            device_id=peer,
            device_id_type=MESH,
        )


def kernel(
    dims,
    act_ref, saved_ref, grad_ref, fids_ref, bids_ref, fgate_ref, bgate_ref, gain_ref,
    wg_hbm, wu_hbm, wd_hbm,
    act_out, grad_out, wgrad,
    wg, wu, wd, xb, xf, gates, rank, left, right, slot, outf, rs_slot, rs_outf, lay, inp,
    send_sems, recv_sems, w_sems,
):
    n_e, n_z, n_s, cap = dims
    tok, width = act_ref.shape
    hid = wg.shape[1]
    topk = fids_ref.shape[1]
    e = lax.axis_index("expert")
    z = lax.axis_index("dp")
    s = lax.axis_index("section")
    t_all = n_e * tok
    slots = n_e * cap
    blk = width // n_z
    cp = Copies(send_sems, recv_sems)
    sent = []

    loads = [
        pltpu.make_async_copy(a, b, w_sems.at[i])
        for i, (a, b) in enumerate(((wg_hbm, wg), (wu_hbm, wu), (wd_hbm, wd)))
    ]
    barrier = pltpu.get_barrier_semaphore()
    peers = [{"expert": e ^ b} for b in bits_of(n_e)]
    peers += [{"dp": lax.rem(z + o, n_z)} for o in range(1, n_z)]
    nxt = {"section": lax.rem(s + 1, n_s)}
    prv = {"section": lax.rem(s + n_s - 1, n_s)}
    peers += [nxt] if n_s == 2 else [nxt, prv]
    for peer in peers:
        pl.semaphore_signal(barrier, inc=1, device_id=peer, device_id_type=MESH)
    for c in loads:
        c.start()

    def rows(b):
        return pl.ds(pl.multiple_of(b * tok, tok), tok)

    def zrows(src):
        return pl.ds(pl.multiple_of(src * t_all, t_all), t_all)

    def lrows(src_z, src_e):
        return pl.ds(pl.multiple_of((src_z * n_e + src_e) * tok, tok), tok)

    def cols(d):
        return pl.ds(pl.multiple_of(d * blk, blk), blk)

    gain = gain_ref[...]

    def factor(x):
        return lax.rsqrt(jnp.mean(x * x, axis=1, keepdims=True) + EPS)

    saved = saved_ref[...].astype(F32)
    xb[0, rows(e), :] = (saved * factor(saved) * gain).astype(BF16)
    xb[1, rows(e), :] = grad_ref[...]
    act = act_ref[...].astype(F32)
    xf[rows(e), :] = (act * factor(act) * gain).astype(BF16)
    lane = lax.broadcasted_iota(jnp.int32, (tok, 128), 1)
    g = jnp.zeros((tok, 128), F32)
    hit = jnp.zeros((tok, 128), F32)
    for k in range(topk):
        g += jnp.where(lane == fids_ref[:, k : k + 1], fgate_ref[:, k : k + 1], 0.0)
        g += jnp.where(lane == bids_ref[:, k : k + 1] + 64, bgate_ref[:, k : k + 1], 0.0)
        hit += jnp.where(lane == bids_ref[:, k : k + 1], 1.0, 0.0)
    gates[rows(e), :] = g
    tri = (
        lax.broadcasted_iota(jnp.int32, (tok, tok), 0)
        >= lax.broadcasted_iota(jnp.int32, (tok, tok), 1)
    ).astype(F32).astype(BF16)
    upto = jnp.dot(tri, hit.astype(BF16), preferred_element_type=F32)
    rank[lrows(z, e), :] = (hit * upto).astype(BF16)

    pl.semaphore_wait(barrier, len(peers))

    def spread(name, ref, m):
        below = [b for b in bits_of(n_e) if m == 0 or b < lowest(m)]
        for b in below:
            c = cp.make((name, m, b), ref(e ^ m), ref(e ^ m), {"expert": e ^ b})
            c.start()
            sent.append(c)

    def arrived(name, ref, m):
        b = lowest(m)
        cp.make((name, m ^ b, b), ref(e ^ m), ref(e ^ m), {"expert": e ^ b}).wait_recv()

    def ref_b(b):
        return xb.at[:, rows(b), :]

    def ref_f(b):
        return xf.at[rows(b), :]

    def ref_g(b):
        return gates.at[rows(b), :]

    order = arrival_order(n_e)
    spread("g", ref_g, 0)
    spread("b", ref_b, 0)
    for o in range(1, n_z):
        d = lax.rem(z + o, n_z)
        for name, src, dst in (
            ("l", xb.at[:, rows(e), cols(d)], left.at[:, lrows(z, e), :]),
            ("r", rank.at[lrows(z, e), :], rank.at[lrows(z, e), :]),
        ):
            c = cp.make((name, "z", o), src, dst, {"dp": d})
            c.start()
            sent.append(c)

    for i, m in enumerate(order):
        arrived("g", ref_g, m)
        spread("g", ref_g, m)
        arrived("b", ref_b, m)
        spread("b", ref_b, m)
        if i == 0:
            spread("f", ref_f, 0)

    def ref_r0(b):
        return rank.at[lrows(z, b), :]

    spread("r0", ref_r0, 0)
    for m in order:
        arrived("r0", ref_r0, m)
        spread("r0", ref_r0, m)
    for c in loads:
        c.wait()

    lanes = lax.broadcasted_iota(jnp.int32, (t_all, 128), 1)

    def column(v, which):
        return jnp.sum(jnp.where(lanes == which, v, 0.0), axis=1, keepdims=True)

    def one_hot(src):
        r = column(rank[zrows(src), :].astype(F32), e)
        at = lax.broadcasted_iota(jnp.int32, (t_all, slots), 1)
        block = lax.broadcasted_iota(jnp.int32, (t_all, slots), 0) // tok
        want = r.astype(jnp.int32) - 1 + block * cap
        return jnp.where((at == want) & (r > 0.5), 1.0, 0.0).astype(BF16)

    gb = column(gates[...], e + 64)
    nb = xb[0]
    pg = jnp.dot(nb, wg[...], preferred_element_type=F32)
    pu = jnp.dot(nb, wu[...], preferred_element_type=F32)
    hg = gb * lax.dot_general(xb[1], wd[...], LAST, preferred_element_type=F32)
    sig = 1.0 / (1.0 + jnp.exp(-pg))
    silu = pg * sig
    gg = (hg * pu * sig * (1.0 + pg * (1.0 - sig))).astype(BF16)
    ug = (hg * silu).astype(BF16)
    hb = (gb * silu * pu).astype(BF16)
    own = one_hot(z)
    for i, v in enumerate((gg, ug, hb)):
        right[z, i] = lax.dot_general(own, v, FIRST, preferred_element_type=F32).astype(BF16)

    def pass_on(way, hop, i, start):
        src = z - hop * way
        if start:
            ok = (z + way >= 0) & (z + way < n_z) & (src >= 0) & (src < n_z)
            peer = z + way
        else:
            ok = (src - way >= 0) & (src - way < n_z) & (z + way >= 0)
            peer = z + way
        src = jnp.clip(src, 0, n_z - 1)
        peer = jnp.clip(peer, 0, n_z - 1)
        return ok, cp.make(
            ("x", way, hop, i), right.at[src, i], right.at[src, i], {"dp": peer}
        )

    relayed = []

    def relay_start(hop):
        for i in range(3):
            for way in (1, -1):
                ok, c = pass_on(way, hop, i, True)
                pl.when(ok)(c.start)
                relayed.append((ok, c))

    def relay_wait(hop):
        for i in range(3):
            for way in (1, -1):
                src = z - hop * way
                ok = (src >= 0) & (src < n_z)
                at = jnp.clip(src, 0, n_z - 1)
                c = cp.make(
                    ("x", way, hop - 1, i), right.at[at, i], right.at[at, i],
                    {"dp": jnp.clip(z + way, 0, n_z - 1)},
                )
                pl.when(ok)(c.wait_recv)

    relay_start(0)

    half = 512
    for j in range(width // half):
        at = slice(j * half, (j + 1) * half)
        v = lax.dot_general(gg, wg[at, :], LAST, preferred_element_type=F32)
        v += lax.dot_general(ug, wu[at, :], LAST, preferred_element_type=F32)
        slot[:, at] = v.astype(BF16)

    def blocks(b):
        return [m for m in range(0, n_e, 2 * b)]

    def place(b):
        return sum(len(blocks(c)) for c in bits_of(n_e) if c < b)

    def reduce_send(name, part, land, b):
        for i, m in enumerate(blocks(b)):
            c = cp.make(
                (name, b, m), part.at[rows(e ^ b ^ m), :], land.at[place(b) + i],
                {"expert": e ^ b},
            )
            c.start()
            sent.append(c)

    def reduce_wait(name, part, land, b):
        for i, m in enumerate(blocks(b)):
            to = land.at[place(b) + i]
            cp.make((name, b, m), part.at[rows(e ^ b ^ m), :], to, {"expert": e ^ b}).wait_recv()

    def reduce_add(part, land, b):
        for i, m in enumerate(blocks(b)):
            v = part[rows(e ^ m), :].astype(F32) + land[place(b) + i].astype(F32)
            part[rows(e ^ m), :] = v.astype(BF16)

    up = list(reversed(bits_of(n_e)))
    reduce_send("s", slot, rs_slot, up[0])

    for m in order:
        arrived("f", ref_f, m)
        spread("f", ref_f, m)
    gf = column(gates[...], e)
    nf = xf[...]
    fg = jnp.dot(nf, wg[...], preferred_element_type=F32)
    fu = jnp.dot(nf, wu[...], preferred_element_type=F32)
    hf = (gf * (fg / (1.0 + jnp.exp(-fg))) * fu).astype(BF16)
    for j in range(width // half):
        at = slice(j * half, (j + 1) * half)
        outf[:, at] = jnp.dot(hf, wd[:, at], preferred_element_type=F32).astype(BF16)
    reduce_send("o", outf, rs_outf, up[0])
    for b, nb_ in zip(up[:-1], up[1:]):
        for name, part, land in (("s", slot, rs_slot), ("o", outf, rs_outf)):
            reduce_wait(name, part, land, b)
            reduce_add(part, land, b)
            reduce_send(name, part, land, nb_)

    def ref_l(o):
        return lambda b: left.at[:, lrows(lax.rem(z + n_z - o, n_z), b), :]

    def ref_r(o):
        return lambda b: rank.at[lrows(lax.rem(z + n_z - o, n_z), b), :]

    for o in range(1, n_z):
        d = lax.rem(z + o, n_z)
        cp.make(
            ("l", "z", o), xb.at[:, rows(e), cols(d)], ref_l(o)(e), {"dp": d}
        ).wait_recv()
        cp.make(("r", "z", o), rank.at[lrows(z, e), :], ref_r(o)(e), {"dp": d}).wait_recv()
        spread(("l", o), ref_l(o), 0)
        spread(("r", o), ref_r(o), 0)

    left[:, zrows(z), :] = xb[:, :, cols(z)]
    scale = 1.0 / n_z

    def add(src, first=False):
        p = one_hot(src)
        for i in range(3):
            at = slice(i * hid, (i + 1) * hid)
            r = jnp.dot(p, right[src, i], preferred_element_type=F32).astype(BF16)
            v = lax.dot_general(
                left[i // 2, zrows(src), :], r, FIRST, preferred_element_type=F32
            ) * scale
            wgrad[:, at] = v if first else wgrad[:, at] + v

    add(z, True)
    relay_wait(1)
    if n_z > 2:
        relay_start(1)

    last = up[-1]
    reduce_wait("s", slot, rs_slot, last)
    ng = (slot[rows(e), :].astype(F32) + rs_slot[place(last)].astype(F32)) * gain
    x = saved_ref[...].astype(F32)
    f = factor(x)
    dot = jnp.mean(x * ng, axis=1, keepdims=True)
    inp[...] = (grad_ref[...].astype(F32) + f * ng - x * (f * f * f * dot)).astype(BF16)
    c_in = cp.make("grad", inp, grad_out, prv)
    c_in.start()
    reduce_wait("o", outf, rs_outf, last)
    lay[...] = (
        act_ref[...].astype(F32)
        + outf[rows(e), :].astype(F32)
        + rs_outf[place(last)].astype(F32)
    ).astype(BF16)
    c_act = cp.make("act", lay, act_out, nxt)
    c_act.start()

    for m in order:
        for o in range(1, n_z):
            for name, ref in (("l", ref_l), ("r", ref_r)):
                arrived((name, o), ref(o), m)
                spread((name, o), ref(o), m)

    for hop in range(1, n_z):
        if hop > 1:
            relay_wait(hop)
            if hop < n_z - 1:
                relay_start(hop)
        for way in (1, -1):
            src = z - hop * way

            @pl.when((src >= 0) & (src < n_z))
            def _():
                add(jnp.clip(src, 0, n_z - 1))

    c_in.wait()
    c_act.wait()
    for c in sent:
        c.wait_send()
    for ok, c in relayed:
        pl.when(ok)(c.wait_send)


def shards(*args):
    n_e, n_z, n_s = (lax.axis_size(a) for a in ("expert", "dp", "section"))
    (act, saved, grad, fids, bids, fgate, bgate) = (a[0] for a in args[:7])
    gain = args[7]
    wg, wu, wd = (a[0, 0] for a in args[8:])
    tok, width = act.shape
    hid = wg.shape[1]
    topk = fids.shape[1]
    cap = min(tok, 5 * tok * topk // (4 * n_e))
    t_all = n_e * tok
    blk = width // n_z
    steps = n_e.bit_length() - 1
    n_copies = 4 * (n_e - 1) + (n_z - 1) * 2 * n_e + 6 * (n_z - 1) + 2 * (n_e - 1) + 2 + steps
    vmem = pl.BlockSpec(memory_space=pltpu.VMEM)
    hbm = pl.BlockSpec(memory_space=pl.ANY)
    act_out, grad_out, wgrad = pl.pallas_call(
        functools.partial(kernel, (n_e, n_z, n_s, cap)),
        out_shape=(
            jax.ShapeDtypeStruct((tok, width), BF16),
            jax.ShapeDtypeStruct((tok, width), BF16),
            jax.ShapeDtypeStruct((blk, 3 * hid), F32),
        ),
        in_specs=[vmem] * 8 + [hbm] * 3,
        out_specs=[vmem] * 3,
        scratch_shapes=[
            pltpu.VMEM((width, hid), BF16),
            pltpu.VMEM((width, hid), BF16),
            pltpu.VMEM((hid, width), BF16),
            pltpu.VMEM((2, t_all, width), BF16),
            pltpu.VMEM((t_all, width), BF16),
            pltpu.VMEM((t_all, 128), F32),
            pltpu.VMEM((n_z * t_all, 128), BF16),
            pltpu.VMEM((2, n_z * t_all, blk), BF16),
            pltpu.VMEM((n_z, 3, n_e * cap, hid), BF16),
            pltpu.VMEM((t_all, width), BF16),
            pltpu.VMEM((t_all, width), BF16),
            pltpu.VMEM((n_e - 1, tok, width), BF16),
            pltpu.VMEM((n_e - 1, tok, width), BF16),
            pltpu.VMEM((tok, width), BF16),
            pltpu.VMEM((tok, width), BF16),
            pltpu.SemaphoreType.DMA((n_copies,)),
            pltpu.SemaphoreType.DMA((n_copies,)),
            pltpu.SemaphoreType.DMA((3,)),
        ],
        compiler_params=pltpu.CompilerParams(
            collective_id=0, has_side_effects=True, vmem_limit_bytes=60 * 1024 * 1024
        ),
    )(act, saved, grad, fids, bids, fgate, bgate, gain, wg, wu, wd)
    return act_out[None], grad_out[None], wgrad[None, None]


def solution(mesh):
    tokens = P("section", ("dp", "expert"), None)
    weights = P("section", "expert", None, None)
    in_specs = (tokens,) * 7 + (P("section", None),) + (weights,) * 3
    out_specs = (tokens, tokens, P("section", "expert", "dp", None))
    return jax.shard_map(shards, mesh=mesh, in_specs=in_specs, out_specs=out_specs, check_vma=False)
```

```python
import functools

import jax
import jax.numpy as jnp
from jax import lax
from jax.experimental import pallas as pl
from jax.experimental.pallas import tpu as pltpu
from jax.sharding import PartitionSpec as P

EPS = 1e-06
MESH = pl.DeviceIdType.MESH
F32 = jnp.float32
BF16 = jnp.bfloat16
LAST = (((1,), (1,)), ((), ()))
FIRST = (((0,), (0,)), ((), ()))


def bits_of(n):
    return [1 << b for b in reversed(range(n.bit_length() - 1))]


def lowest(m):
    return m & -m


def arrival_order(n):
    return sorted(range(1, n), key=lambda m: (-lowest(m), m))


class Copies:
    def __init__(self, send, recv):
        self.send, self.recv, self.names = send, recv, {}

    def make(self, name, src, dst, peer):
        i = self.names.setdefault(name, len(self.names))
        return pltpu.make_async_remote_copy(
            src_ref=src,
            dst_ref=dst,
            send_sem=self.send.at[i],
            recv_sem=self.recv.at[i],
            device_id=peer,
            device_id_type=MESH,
        )


def kernel(
    dims,
    act_ref, saved_ref, grad_ref, fids_ref, bids_ref, fgate_ref, bgate_ref, gain_ref,
    wg_hbm, wu_hbm, wd_hbm,
    act_out, grad_out, wgrad,
    wg, wu, wd, xb, xf, gates, rank, left, right, slot, outf, rs_slot, rs_outf, lay, inp,
    send_sems, recv_sems, w_sems,
):
    n_e, n_z, n_s, cap = dims
    tok, width = act_ref.shape
    hid = wg.shape[1]
    topk = fids_ref.shape[0]
    e = lax.axis_index("expert")
    z = lax.axis_index("dp")
    s = lax.axis_index("section")
    t_all = n_e * tok
    slots = n_e * cap
    blk = width // n_z
    cp = Copies(send_sems, recv_sems)
    sent = []

    loads = [
        pltpu.make_async_copy(a, b, w_sems.at[i])
        for i, (a, b) in enumerate(((wg_hbm, wg), (wu_hbm, wu), (wd_hbm, wd)))
    ]
    barrier = pltpu.get_barrier_semaphore()
    peers = [{"expert": e ^ b} for b in bits_of(n_e)]
    peers += [{"dp": lax.rem(z + o, n_z)} for o in range(1, n_z)]
    nxt = {"section": lax.rem(s + 1, n_s)}
    prv = {"section": lax.rem(s + n_s - 1, n_s)}
    peers += [nxt] if n_s == 2 else [nxt, prv]
    for peer in peers:
        pl.semaphore_signal(barrier, inc=1, device_id=peer, device_id_type=MESH)
    for c in loads:
        c.start()

    def rows(b):
        return pl.ds(pl.multiple_of(b * tok, tok), tok)

    def zrows(src):
        return pl.ds(pl.multiple_of(src * t_all, t_all), t_all)

    def lrows(src_z, src_e):
        return pl.ds(pl.multiple_of((src_z * n_e + src_e) * tok, tok), tok)

    def cols(d):
        return pl.ds(pl.multiple_of(d * blk, blk), blk)

    gain = gain_ref[...]

    def factor(x):
        return lax.rsqrt(jnp.mean(x * x, axis=1, keepdims=True) + EPS)

    saved = saved_ref[...].astype(F32)
    xb[0, rows(e), :] = (saved * factor(saved) * gain).astype(BF16)
    xb[1, rows(e), :] = grad_ref[...]
    act = act_ref[...].astype(F32)
    xf[rows(e), :] = (act * factor(act) * gain).astype(BF16)
    lane = lax.broadcasted_iota(jnp.int32, (tok, 128), 1)
    g = jnp.zeros((tok, 128), F32)
    hit = jnp.zeros((tok, 128), F32)
    down = lax.broadcasted_iota(jnp.int32, (tok, tok), 0)
    across = lax.broadcasted_iota(jnp.int32, (tok, tok), 1)

    def turned(ref, k):
        row = ref[k : k + 1, :].astype(F32)
        return jnp.sum(jnp.where(down == across, row, 0.0), axis=1, keepdims=True)

    for k in range(topk):
        f_id = turned(fids_ref, k).astype(jnp.int32)
        b_id = turned(bids_ref, k).astype(jnp.int32)
        g += jnp.where(lane == f_id, turned(fgate_ref, k), 0.0)
        g += jnp.where(lane == b_id + 64, turned(bgate_ref, k), 0.0)
        hit += jnp.where(lane == b_id, 1.0, 0.0)
    gates[rows(e), :] = g
    tri = (down >= across).astype(F32).astype(BF16)
    upto = jnp.dot(tri, hit.astype(BF16), preferred_element_type=F32)
    rank[lrows(z, e), :] = (hit * upto).astype(BF16)

    pl.semaphore_wait(barrier, len(peers))

    def spread(name, ref, m):
        below = [b for b in bits_of(n_e) if m == 0 or b < lowest(m)]
        for b in below:
            c = cp.make((name, m, b), ref(e ^ m), ref(e ^ m), {"expert": e ^ b})
            c.start()
            sent.append(c)

    def arrived(name, ref, m):
        b = lowest(m)
        cp.make((name, m ^ b, b), ref(e ^ m), ref(e ^ m), {"expert": e ^ b}).wait_recv()

    def ref_b(i):
        return lambda b: xb.at[i, rows(b), :]

    def ref_f(b):
        return xf.at[rows(b), :]

    def ref_g(b):
        return gates.at[rows(b), :]

    order = arrival_order(n_e)
    spread("g", ref_g, 0)
    spread(("b", 1), ref_b(1), 0)
    spread(("b", 0), ref_b(0), 0)
    for o in range(1, n_z):
        d = lax.rem(z + o, n_z)
        for name, src, dst in (
            ("l", xb.at[:, rows(e), cols(d)], left.at[:, lrows(z, e), :]),
            ("r", rank.at[lrows(z, e), :], rank.at[lrows(z, e), :]),
        ):
            c = cp.make((name, "z", o), src, dst, {"dp": d})
            c.start()
            sent.append(c)

    for i, m in enumerate(order):
        arrived("g", ref_g, m)
        spread("g", ref_g, m)
        for a in (1, 0):
            arrived(("b", a), ref_b(a), m)
            spread(("b", a), ref_b(a), m)
        if i == 0:
            spread("f", ref_f, 0)

    def ref_r0(b):
        return rank.at[lrows(z, b), :]

    spread("r0", ref_r0, 0)
    for m in order:
        arrived("r0", ref_r0, m)
        spread("r0", ref_r0, m)
    def ref_l(o):
        return lambda b: left.at[:, lrows(lax.rem(z + n_z - o, n_z), b), :]

    def ref_r(o):
        return lambda b: rank.at[lrows(lax.rem(z + n_z - o, n_z), b), :]

    for o in range(1, n_z):
        d = lax.rem(z + o, n_z)
        cp.make(
            ("l", "z", o), xb.at[:, rows(e), cols(d)], ref_l(o)(e), {"dp": d}
        ).wait_recv()
        cp.make(("r", "z", o), rank.at[lrows(z, e), :], ref_r(o)(e), {"dp": d}).wait_recv()
        spread(("l", o), ref_l(o), 0)
        spread(("r", o), ref_r(o), 0)

    for c in loads:
        c.wait()

    lanes = lax.broadcasted_iota(jnp.int32, (t_all, 128), 1)

    def column(v, which):
        return jnp.sum(jnp.where(lanes == which, v, 0.0), axis=1, keepdims=True)

    def one_hot(src):
        r = column(rank[zrows(src), :].astype(F32), e)
        at = lax.broadcasted_iota(jnp.int32, (t_all, slots), 1)
        block = lax.broadcasted_iota(jnp.int32, (t_all, slots), 0) // tok
        want = r.astype(jnp.int32) - 1 + block * cap
        return jnp.where((at == want) & (r > 0.5), 1.0, 0.0).astype(BF16)

    gb = column(gates[...], e + 64)
    nb = xb[0]
    pg = jnp.dot(nb, wg[...], preferred_element_type=F32)
    pu = jnp.dot(nb, wu[...], preferred_element_type=F32)
    hg = gb * lax.dot_general(xb[1], wd[...], LAST, preferred_element_type=F32)
    sig = 1.0 / (1.0 + jnp.exp(-pg))
    silu = pg * sig
    gg = (hg * pu * sig * (1.0 + pg * (1.0 - sig))).astype(BF16)
    ug = (hg * silu).astype(BF16)
    hb = (gb * silu * pu).astype(BF16)
    own = one_hot(z)
    for i, v in enumerate((gg, ug, hb)):
        right[z, i] = lax.dot_general(own, v, FIRST, preferred_element_type=F32).astype(BF16)

    def pass_on(way, hop, i):
        src = z - hop * way
        peer = z + way
        ok = (peer >= 0) & (peer < n_z) & (src >= 0) & (src < n_z)
        src = jnp.clip(src, 0, n_z - 1)
        peer = jnp.clip(peer, 0, n_z - 1)
        return ok, cp.make(
            ("x", way, hop, i), right.at[src, i], right.at[src, i], {"dp": peer}
        )

    relayed = []

    def relay(hop):
        for i in range(3):
            for way in (1, -1):
                if hop > 0:
                    src = z - hop * way
                    at = jnp.clip(src, 0, n_z - 1)
                    here = cp.make(
                        ("x", way, hop - 1, i), right.at[at, i], right.at[at, i],
                        {"dp": jnp.clip(z + way, 0, n_z - 1)},
                    )
                    pl.when((src >= 0) & (src < n_z))(here.wait_recv)
                if hop < n_z - 1:
                    ok, c = pass_on(way, hop, i)
                    pl.when(ok)(c.start)
                    relayed.append((ok, c))

    relay(0)

    half = 512
    for j in range(width // half):
        at = slice(j * half, (j + 1) * half)
        v = lax.dot_general(gg, wg[at, :], LAST, preferred_element_type=F32)
        v += lax.dot_general(ug, wu[at, :], LAST, preferred_element_type=F32)
        slot[:, at] = v.astype(BF16)

    def blocks(b):
        return [m for m in range(0, n_e, 2 * b)]

    def place(b):
        return sum(len(blocks(c)) for c in bits_of(n_e) if c < b)

    def reduce_send(name, part, land, b):
        for i, m in enumerate(blocks(b)):
            c = cp.make(
                (name, b, m), part.at[rows(e ^ b ^ m), :], land.at[place(b) + i],
                {"expert": e ^ b},
            )
            c.start()
            sent.append(c)

    def reduce_wait(name, part, land, b):
        for i, m in enumerate(blocks(b)):
            to = land.at[place(b) + i]
            cp.make((name, b, m), part.at[rows(e ^ b ^ m), :], to, {"expert": e ^ b}).wait_recv()

    def reduce_add(part, land, b):
        for i, m in enumerate(blocks(b)):
            v = part[rows(e ^ m), :].astype(F32) + land[place(b) + i].astype(F32)
            part[rows(e ^ m), :] = v.astype(BF16)

    up = list(reversed(bits_of(n_e)))
    reduce_send("s", slot, rs_slot, up[0])

    for m in order:
        arrived("f", ref_f, m)
        spread("f", ref_f, m)
    gf = column(gates[...], e)
    nf = xf[...]
    fg = jnp.dot(nf, wg[...], preferred_element_type=F32)
    fu = jnp.dot(nf, wu[...], preferred_element_type=F32)
    hf = (gf * (fg / (1.0 + jnp.exp(-fg))) * fu).astype(BF16)
    for j in range(width // half):
        at = slice(j * half, (j + 1) * half)
        outf[:, at] = jnp.dot(hf, wd[:, at], preferred_element_type=F32).astype(BF16)
    reduce_send("o", outf, rs_outf, up[0])
    for b, nb_ in zip(up[:-1], up[1:]):
        for name, part, land in (("s", slot, rs_slot), ("o", outf, rs_outf)):
            reduce_wait(name, part, land, b)
            reduce_add(part, land, b)
            reduce_send(name, part, land, nb_)

    left[:, zrows(z), :] = xb[:, :, cols(z)]
    scale = 1.0 / n_z

    def add(src, first=False):
        p = one_hot(src)
        for i in range(3):
            at = slice(i * hid, (i + 1) * hid)
            r = jnp.dot(p, right[src, i], preferred_element_type=F32).astype(BF16)
            v = lax.dot_general(
                left[i // 2, zrows(src), :], r, FIRST, preferred_element_type=F32
            ) * scale
            wgrad[:, at] = v if first else wgrad[:, at] + v

    relay(1)
    add(z, True)
    for m in order:
        for o in range(1, n_z):
            for name, ref in (("l", ref_l), ("r", ref_r)):
                arrived((name, o), ref(o), m)
                spread((name, o), ref(o), m)

    last = up[-1]
    reduce_wait("s", slot, rs_slot, last)
    ng = (slot[rows(e), :].astype(F32) + rs_slot[place(last)].astype(F32)) * gain
    x = saved_ref[...].astype(F32)
    f = factor(x)
    dot = jnp.mean(x * ng, axis=1, keepdims=True)
    inp[...] = (grad_ref[...].astype(F32) + f * ng - x * (f * f * f * dot)).astype(BF16)
    c_in = cp.make("grad", inp, grad_out, prv)
    c_in.start()
    reduce_wait("o", outf, rs_outf, last)
    lay[...] = (
        act_ref[...].astype(F32)
        + outf[rows(e), :].astype(F32)
        + rs_outf[place(last)].astype(F32)
    ).astype(BF16)
    c_act = cp.make("act", lay, act_out, nxt)
    c_act.start()

    if n_z > 3:
        relay(2)
    for hop in range(1, n_z):
        if hop > 2 or hop == n_z - 1 > 1:
            relay(hop)
        for way in (1, -1):
            src = z - hop * way

            @pl.when((src >= 0) & (src < n_z))
            def _():
                add(jnp.clip(src, 0, n_z - 1))

    c_in.wait()
    c_act.wait()
    for c in sent:
        c.wait_send()
    for ok, c in relayed:
        pl.when(ok)(c.wait_send)


def copy_kernel(*refs):
    n = len(refs) // 2
    for src, dst in zip(refs[:n], refs[n:]):
        dst[...] = src[...]


def hand_on(*arrays):
    steps = 4
    specs = [pl.BlockSpec((a.shape[0] // steps, a.shape[1]), lambda i: (i, 0)) for a in arrays]
    return pl.pallas_call(
        copy_kernel,
        out_shape=tuple(jax.ShapeDtypeStruct(a.shape, a.dtype) for a in arrays),
        grid=(steps,),
        in_specs=specs,
        out_specs=specs,
    )(*arrays)


def shards(*args):
    n_e, n_z, n_s = (lax.axis_size(a) for a in ("expert", "dp", "section"))
    (act, saved, grad, fids, bids, fgate, bgate) = (a[0] for a in args[:7])
    gain = args[7]
    wg, wu, wd = (a[0, 0] for a in args[8:])
    tok, width = act.shape
    hid = wg.shape[1]
    topk = fids.shape[1]
    small = [a.T for a in (fids, bids, fgate, bgate)]
    cap = min(tok, 5 * tok * topk // (4 * n_e))
    t_all = n_e * tok
    blk = width // n_z
    steps = n_e.bit_length() - 1
    n_copies = 5 * (n_e - 1) + (n_z - 1) * 2 * n_e + 6 * (n_z - 1) + 2 * (n_e - 1) + 2 + steps
    vmem = pl.BlockSpec(memory_space=pltpu.VMEM)
    hbm = pl.BlockSpec(memory_space=pl.ANY)
    act_out, grad_out, wgrad = pl.pallas_call(
        functools.partial(kernel, (n_e, n_z, n_s, cap)),
        out_shape=(
            jax.ShapeDtypeStruct((tok, width), BF16),
            jax.ShapeDtypeStruct((tok, width), BF16),
            jax.ShapeDtypeStruct((blk, 3 * hid), F32),
        ),
        in_specs=[vmem] * 8 + [hbm] * 3,
        out_specs=[vmem] * 3,
        scratch_shapes=[
            pltpu.VMEM((width, hid), BF16),
            pltpu.VMEM((width, hid), BF16),
            pltpu.VMEM((hid, width), BF16),
            pltpu.VMEM((2, t_all, width), BF16),
            pltpu.VMEM((t_all, width), BF16),
            pltpu.VMEM((t_all, 128), F32),
            pltpu.VMEM((n_z * t_all, 128), BF16),
            pltpu.VMEM((2, n_z * t_all, blk), BF16),
            pltpu.VMEM((n_z, 3, n_e * cap, hid), BF16),
            pltpu.VMEM((t_all, width), BF16),
            pltpu.VMEM((t_all, width), BF16),
            pltpu.VMEM((n_e - 1, tok, width), BF16),
            pltpu.VMEM((n_e - 1, tok, width), BF16),
            pltpu.VMEM((tok, width), BF16),
            pltpu.VMEM((tok, width), BF16),
            pltpu.SemaphoreType.DMA((n_copies,)),
            pltpu.SemaphoreType.DMA((n_copies,)),
            pltpu.SemaphoreType.DMA((3,)),
        ],
        compiler_params=pltpu.CompilerParams(
            collective_id=0, has_side_effects=True, vmem_limit_bytes=60 * 1024 * 1024
        ),
    )(act, saved, grad, *small, gain, wg, wu, wd)
    act_out, grad_out, wgrad = hand_on(act_out, grad_out, wgrad)
    return act_out[None], grad_out[None], wgrad[None, None]


def solution(mesh):
    tokens = P("section", ("dp", "expert"), None)
    weights = P("section", "expert", None, None)
    in_specs = (tokens,) * 7 + (P("section", None),) + (weights,) * 3
    out_specs = (tokens, tokens, P("section", "expert", "dp", None))
    return jax.shard_map(shards, mesh=mesh, in_specs=in_specs, out_specs=out_specs, check_vma=False)
```
